128 devices in a mesh: dp: 16 (over z, y_hi, core), tensor: 8 (over x, y_lo).
Axes of the slice: x: 4, y: 4 (y_hi: 2, y_lo: 2; y = y_hi * 2 + y_lo), z: 4, core: 2. Of those that a mesh axis runs over, the one named last changes fastest.
Arguments:
- activations: bfloat16 [1024, 4608], P('dp', 'tensor'), may hold values from -6 to 6
- enc_weight: bfloat16 [4608, 65536], P(None, ('dp', 'tensor')), may hold values from -0.09375 to 0.09375
- enc_bias: float32 [65536], P(('dp', 'tensor')), may hold values from -3 to 3
- thresholds: float32 [65536], P(('dp', 'tensor')), may hold values from 0.1 to 1
- dec_weight: bfloat16 [65536, 4608], P(('dp', 'tensor')), may hold values from -0.0234375 to 0.0234375
- dec_bias: float32 [4608], replicated, may hold values from -3 to 3
Outputs:
- grad_enc: bfloat16 [4608, 65536], P(None, ('dp', 'tensor'))
- grad_dec: bfloat16 [65536, 4608], P(('dp', 'tensor'))
The draws below stay inside these ranges and needn't reach their ends.
All inputs are finite; a program needn't handle non-finite values.
Results may differ from the reference program's by a relative error of at most 0.0075.
Values may be sent and summed in bfloat16 or wider, within the bound.
No kernel may reach another device: no remote copies, remote signals or barrier semaphores. Data moves between devices by JAX's collectives and lax.ppermute only.
A program may use at most 128 MiB of HBM per device.

```python
import math
import jax
import jax.numpy as jnp
from jax import lax

D = 4608
LATENTS = 65536
TOKENS = 1024


def level_of(rng, extent, pieces, smallest, top_value):
    level, own = 1.0, jax.random.fold_in(rng, 6)
    for position, parts in pieces:
        steps = jnp.exp(jax.random.uniform(jax.random.fold_in(own, position), (parts,), jnp.float32, smallest / len(pieces), top_value / len(pieces)))
        level = level * jnp.repeat(steps, extent[position] // parts).reshape([-1 if axis == position else 1 for axis in range(len(extent))])
    return level


def bell_draw(key, extent, deviation, limit, cuts=(), kind=jnp.bfloat16):
    result = deviation * jax.random.normal(key, extent, jnp.float32)
    if cuts:
        result = result * level_of(key, extent, cuts, -0.22, 0.18)
    return jnp.clip(result, -limit, limit).astype(kind)


def setup_inputs(seed: int = 0) -> dict:
    splits = jax.random.split(jax.random.key(seed), 7)
    return {
        "activations": bell_draw(splits[0], (TOKENS, D), 1.0, 6.0, ((0, 16), (1, 8))),
        "enc_weight": bell_draw(splits[1], (D, LATENTS), D ** -0.5, 0.09375, ((1, 128),)),
        "enc_bias": bell_draw(splits[2], (LATENTS,), 0.5, 3.0, ((0, 128),), jnp.float32),
        "thresholds": jnp.clip(jnp.exp(math.log(1.0) - 2.3025851 * jax.random.uniform(splits[3], (LATENTS,), jnp.float32) ** level_of(splits[3], (LATENTS,), ((0, 128),), -0.2, 0.2)), 0.1, 1.0),
        "dec_weight": bell_draw(splits[4], (LATENTS, D), LATENTS ** -0.5, 0.0234375, ((0, 128),)),
        "dec_bias": bell_draw(splits[5], (D,), 0.5, 3.0, (), jnp.float32),
    }


band_width = 0.1
sparsity_coeff = 0.5

def reference(activations, enc_weight, enc_bias, thresholds, dec_weight, dec_bias):
    centered = (activations.astype(jnp.float32) - dec_bias).astype(jnp.bfloat16)
    pre_act = jnp.dot(centered, enc_weight, preferred_element_type=jnp.float32) + enc_bias
    gating = jax.nn.sigmoid((pre_act - thresholds) / band_width)
    code_values = pre_act * gating
    code_half = code_values.astype(jnp.bfloat16)
    recon_sum = jnp.dot(code_half, dec_weight, preferred_element_type=jnp.float32)
    recon_error = recon_sum + dec_bias - activations.astype(jnp.float32)
    row_scale = 1.0 / math.sqrt(TOKENS)
    delta_half = (recon_error * row_scale).astype(jnp.bfloat16)
    row_norms = jnp.sqrt(lax.optimization_barrier(jnp.sum(jnp.square(dec_weight.astype(jnp.float32)), axis=1)) + 1e-06)
    code_grad = lax.dot_general(delta_half, dec_weight, (((1,), (1,)), ((), ())), preferred_element_type=jnp.float32)
    code_grad = code_grad + sparsity_coeff * row_scale * row_norms
    slopes = gating + pre_act * gating * (1.0 - gating) / band_width
    preact_grad = (code_grad * slopes).astype(jnp.bfloat16)
    grad_enc = lax.dot_general(centered, preact_grad, (((0,), (0,)), ((), ())), preferred_element_type=jnp.float32)
    totals = lax.optimization_barrier(jnp.sum(code_values, axis=0))
    grad_dec = lax.dot_general(code_half, delta_half, (((0,), (0,)), ((), ())), preferred_element_type=jnp.float32)
    grad_dec = grad_dec + sparsity_coeff * row_scale * totals[:, None] * dec_weight.astype(jnp.float32) / row_norms[:, None]
    return (grad_enc.astype(jnp.bfloat16), grad_dec.astype(jnp.bfloat16))
```

```python
import math

import jax
import jax.numpy as jnp
from jax import lax
from jax.sharding import Mesh, PartitionSpec as P

band_width = 0.1
sparsity_coeff = 0.5

bf16, f32 = jnp.bfloat16, jnp.float32
MESH = ("z", "yh", "core", "x", "yl")


def device(z, y, x, core):
    return (((z * 2 + y // 2) * 2 + core) * 4 + x) * 2 + y % 2


def cubes(pairing):
    groups = []
    for core in range(2):
        step = (1, 3)[(pairing + core) % 2]
        corners = (0, 1 if step == 3 else 2)
        pairs = [(corner, corner ^ step) for corner in corners]
        for zs in pairs:
            for ys in pairs:
                for xs in pairs:
                    groups.append([device(z, y, x, core) for z in zs for y in ys for x in xs])
    return groups


def trade(blocks, pairing):
    return lax.all_to_all(blocks, MESH, 0, 0, axis_index_groups=cubes(pairing))


def swap(block):
    return lax.ppermute(block, "core", [(0, 1), (1, 0)])


def barrier(*arrays):
    return lax.optimization_barrier(arrays)


def gather(own):
    rows = own
    for pairing in (0, 1):
        copies, = barrier(jnp.broadcast_to(rows, (8, *rows.shape)))
        rows = trade(copies, pairing).reshape(-1, own.shape[1])
    rows, = barrier(rows)
    return rows, swap(rows)


def scatter(blocks):
    for pairing in (1, 0):
        blocks = blocks.astype(bf16).reshape(8, -1, blocks.shape[-1])
        blocks = jnp.sum(trade(blocks, pairing).astype(f32), axis=0)
    return blocks


def on_device(activations, enc_weight, enc_bias, thresholds, dec_weight, dec_bias):
    row_scale = 1.0 / math.sqrt(1024)
    own_rows = lax.all_to_all(activations, ("x", "yl"), split_axis=0, concat_axis=1, tiled=True)
    own_rows = own_rows.astype(f32)
    row_norms = jnp.sqrt(jnp.sum(jnp.square(dec_weight.astype(f32)), axis=1) + 1e-06)
    own_centered, = barrier((own_rows - dec_bias).astype(bf16))
    centered = gather(own_centered)

    def encode(rows):
        pre_act, = barrier(jnp.dot(rows, enc_weight, preferred_element_type=f32) + enc_bias)
        gating = jax.nn.sigmoid((pre_act - thresholds) / band_width)
        code_values = pre_act * gating
        slopes = gating + pre_act * gating * (1.0 - gating) / band_width
        return barrier(code_values.astype(bf16), slopes, jnp.sum(code_values, axis=0))

    code, slopes, totals = zip(*(encode(rows) for rows in centered))
    totals = totals[0] + totals[1]

    recon = []
    for part in jnp.split(dec_weight, 3, axis=1):
        theirs = swap(jnp.dot(code[1], part, preferred_element_type=f32).astype(bf16))
        mine = jnp.dot(code[0], part, preferred_element_type=f32)
        recon.append((mine + theirs.astype(f32)).astype(bf16))
    recon, = barrier(jnp.concatenate(recon, axis=1))
    recon_error = scatter(recon) + dec_bias - own_rows
    own_delta, = barrier((recon_error * row_scale).astype(bf16))
    delta = gather(own_delta)

    grads = []
    for rows, code_rows, slope, delta_rows in zip(centered, code, slopes, delta):
        code_grad = lax.dot_general(
            delta_rows, dec_weight, (((1,), (1,)), ((), ())), preferred_element_type=f32
        )
        code_grad = code_grad + sparsity_coeff * row_scale * row_norms
        rows_t, code_t, preact_grad = barrier(rows.T, code_rows.T, (code_grad * slope).astype(bf16))
        grads.append(
            (
                jnp.dot(rows_t, preact_grad, preferred_element_type=f32),
                jnp.dot(code_t, delta_rows, preferred_element_type=f32),
            )
        )
    (grad_enc, grad_dec), (more_enc, more_dec) = grads
    grad_dec = (
        grad_dec
        + sparsity_coeff
        * row_scale
        * totals[:, None]
        * dec_weight.astype(f32)
        / row_norms[:, None]
    )
    grad_enc, grad_dec = barrier(grad_enc, grad_dec)
    return ((grad_enc + more_enc).astype(bf16), (grad_dec + more_dec).astype(bf16))


def solution(mesh):
    torus = Mesh(mesh.devices.reshape(4, 2, 2, 4, 2), MESH)
    dp, tensor = ("z", "yh", "core"), ("x", "yl")
    latents = dp + tensor
    in_specs = (P(dp, tensor), P(None, latents), P(latents), P(latents), P(latents, None), P())
    out_specs = (P(None, latents), P(latents, None))
    return jax.shard_map(
        on_device, mesh=torus, in_specs=in_specs, out_specs=out_specs, check_vma=False
    )
```

```python
import math

import jax
import jax.numpy as jnp
from jax import lax
from jax.sharding import Mesh, PartitionSpec as P

band_width = 0.1
sparsity_coeff = 0.5

bf16, f32 = jnp.bfloat16, jnp.float32
MESH = ("z", "yh", "core", "x", "yl")


def device(z, y, x, core):
    return (((z * 2 + y // 2) * 2 + core) * 4 + x) * 2 + y % 2


def receive(block, axes, pairing):
    pairs = []
    for z in range(4):
        for y in range(4):
            for x in range(4):
                for core in range(2):
                    partner = {"z": z, "y": y, "x": x}
                    for axis in axes:
                        partner[axis] ^= (1, 3)[(pairing + core) % 2]
                    pairs.append((device(core=core, **partner), device(z, y, x, core)))
    return lax.ppermute(block, MESH, pairs)


def cubes(pairing):
    groups = []
    for core in range(2):
        step = (1, 3)[(pairing + core) % 2]
        corners = (0, 1 if step == 3 else 2)
        pairs = [(corner, corner ^ step) for corner in corners]
        for zs in pairs:
            for ys in pairs:
                for xs in pairs:
                    groups.append([device(z, y, x, core) for z in zs for y in ys for x in xs])
    return groups


def trade(blocks, pairing):
    return lax.all_to_all(blocks, MESH, 0, 0, axis_index_groups=cubes(pairing))


def swap(block):
    return lax.ppermute(block, "core", [(0, 1), (1, 0)])


def barrier(*arrays):
    return lax.optimization_barrier(arrays)


def add(*blocks):
    return sum(block.astype(f32) for block in blocks)


def flat(block):
    return block.reshape(-1, block.shape[-1])


def gather(own, work):
    copies, = barrier(jnp.broadcast_to(own, (8, *own.shape)))
    block, = barrier(trade(copies, 0))
    x, y, z, xyz = (receive(block, corner, 1) for corner in ("x", "y", "z", "xyz"))
    near, = barrier(jnp.concatenate([block, x, y, z]))
    xy, yz, zx = receive(y, "x", 1), receive(z, "y", 1), receive(x, "z", 1)
    near, = barrier(jnp.concatenate([near, swap(near)]))
    near = flat(near)
    done = work(near)
    xy, yz, zx, xyz, _ = barrier(xy, yz, zx, xyz, done)
    distant, = barrier(jnp.concatenate([xy, yz, zx, xyz]))
    return near, done, flat(distant), flat(swap(distant))


def scatter(near, distant, work):
    xy, yz, zx, xyz = jnp.split(distant.reshape(32, 8, -1), 4)
    own, x, y, z = jnp.split(near.reshape(32, 8, -1), 4)
    y_more, z_more, x_more = receive(xy, "x", 1), receive(yz, "y", 1), receive(zx, "z", 1)
    xyz = receive(xyz, "xyz", 1)
    x, y, z = (add(*pair).astype(bf16) for pair in ((x, x_more), (y, y_more), (z, z_more)))
    x, y, z = receive(x, "x", 1), receive(y, "y", 1), receive(z, "z", 1)
    x, y, z, xyz, done = barrier(x, y, z, xyz, work)
    blocks = trade(add(own, xyz, x, y, z).astype(bf16), 0)
    return jnp.sum(blocks.astype(f32), axis=0), done


def on_device(activations, enc_weight, enc_bias, thresholds, dec_weight, dec_bias):
    row_scale = 1.0 / math.sqrt(1024)
    own_rows = lax.all_to_all(activations, ("x", "yl"), split_axis=0, concat_axis=1, tiled=True)
    own_rows = own_rows.astype(f32)
    row_norms = jnp.sqrt(jnp.sum(jnp.square(dec_weight.astype(f32)), axis=1) + 1e-06)
    own_centered, = barrier((own_rows - dec_bias).astype(bf16))

    def encode(rows):
        pre_act, = barrier(jnp.dot(rows, enc_weight, preferred_element_type=f32) + enc_bias)
        gating = jax.nn.sigmoid((pre_act - thresholds) / band_width)
        code_values = pre_act * gating
        slopes = gating + pre_act * gating * (1.0 - gating) / band_width
        return barrier(code_values.astype(bf16), slopes, jnp.sum(code_values, axis=0))

    near, encoded, mine, theirs = gather(own_centered, encode)
    code_near, slopes_near, totals_near = encoded
    code_mine, slopes_mine, totals_mine = encode(mine)
    code_theirs, slopes_theirs, totals_theirs = encode(theirs)
    totals = totals_near + totals_mine + totals_theirs

    code_mine_all, code_theirs_all = barrier(
        jnp.concatenate([code_mine, code_near[:256]]),
        jnp.concatenate([code_theirs, code_near[256:]]),
    )
    recon_theirs = jnp.dot(code_theirs_all, dec_weight, preferred_element_type=f32).astype(bf16)
    recon_theirs = swap(recon_theirs[:256]), swap(recon_theirs[256:])
    recon_mine, = barrier(
        jnp.dot(code_mine_all, dec_weight, preferred_element_type=f32).astype(bf16)
    )
    recon_distant, = barrier(add(recon_mine[:256], recon_theirs[0]).astype(bf16))
    recon_mine, recon_distant = barrier(recon_mine, recon_distant)
    recon_near = add(recon_mine[256:], recon_theirs[1]).astype(bf16)
    near_t, code_near_t, distant_t, code_distant_t = (
        near.T,
        code_near.T,
        jnp.concatenate([mine, theirs]).T,
        jnp.concatenate([code_mine, code_theirs]).T,
    )
    slopes_distant = jnp.concatenate([slopes_mine, slopes_theirs])
    recon, (near_t, code_near_t, distant_t, code_distant_t, slopes_distant) = scatter(
        recon_near, recon_distant, (near_t, code_near_t, distant_t, code_distant_t, slopes_distant)
    )
    recon_error = recon + dec_bias - own_rows
    own_delta, = barrier((recon_error * row_scale).astype(bf16))

    def preact_grad(delta, slopes):
        code_grad = lax.dot_general(
            delta, dec_weight, (((1,), (1,)), ((), ())), preferred_element_type=f32
        )
        return barrier(
            ((code_grad + sparsity_coeff * row_scale * row_norms) * slopes).astype(bf16)
        )[0]

    def near_grad(delta):
        return jnp.dot(near_t, preact_grad(delta, slopes_near), preferred_element_type=f32)

    delta_near, grad_enc, mine, theirs = gather(own_delta, near_grad)
    grad_dec = jnp.dot(code_near_t, delta_near, preferred_element_type=f32)
    grad_dec = (
        grad_dec
        + sparsity_coeff
        * row_scale
        * totals[:, None]
        * dec_weight.astype(f32)
        / row_norms[:, None]
    )
    grad_dec, = barrier(grad_dec)
    theirs, _ = barrier(theirs, grad_dec)
    delta, = barrier(jnp.concatenate([mine, theirs]))
    preact = preact_grad(delta, slopes_distant)
    grad_enc = grad_enc + jnp.dot(distant_t, preact, preferred_element_type=f32)
    grad_dec = grad_dec + jnp.dot(code_distant_t, delta, preferred_element_type=f32)
    return (grad_enc.astype(bf16), grad_dec.astype(bf16))


def solution(mesh):
    torus = Mesh(mesh.devices.reshape(4, 2, 2, 4, 2), MESH)
    dp, tensor = ("z", "yh", "core"), ("x", "yl")
    latents = dp + tensor
    in_specs = (P(dp, tensor), P(None, latents), P(latents), P(latents), P(latents, None), P())
    out_specs = (P(None, latents), P(latents, None))
    return jax.shard_map(
        on_device, mesh=torus, in_specs=in_specs, out_specs=out_specs, check_vma=False
    )
```

```python
import math

import jax
import jax.numpy as jnp
from jax import lax
from jax.sharding import Mesh, PartitionSpec as P

band_width = 0.1
sparsity_coeff = 0.5

bf16, f32 = jnp.bfloat16, jnp.float32
MESH = ("z", "yh", "core", "x", "yl")


def device(z, y, x, core):
    return (((z * 2 + y // 2) * 2 + core) * 4 + x) * 2 + y % 2


def receive(block, axes, pairing):
    pairs = []
    for z in range(4):
        for y in range(4):
            for x in range(4):
                for core in range(2):
                    partner = {"z": z, "y": y, "x": x}
                    for axis in axes:
                        partner[axis] ^= (1, 3)[(pairing + core) % 2]
                    pairs.append((device(core=core, **partner), device(z, y, x, core)))
    return lax.ppermute(block, MESH, pairs)


def cubes(pairing):
    groups = []
    for core in range(2):
        step = (1, 3)[(pairing + core) % 2]
        corners = (0, 1 if step == 3 else 2)
        pairs = [(corner, corner ^ step) for corner in corners]
        for zs in pairs:
            for ys in pairs:
                for xs in pairs:
                    groups.append([device(z, y, x, core) for z in zs for y in ys for x in xs])
    return groups


def trade(blocks, pairing):
    return lax.all_to_all(blocks, MESH, 0, 0, axis_index_groups=cubes(pairing))


def swap(block):
    return lax.ppermute(block, "core", [(0, 1), (1, 0)])


def barrier(*arrays):
    return lax.optimization_barrier(arrays)


def add(*blocks):
    return sum(block.astype(f32) for block in blocks)


def flat(block):
    return block.reshape(-1, block.shape[-1])


def gather(own, work):
    copies, = barrier(jnp.broadcast_to(own, (8, *own.shape)))
    block, = barrier(trade(copies, 0))
    x, y, z, xyz = (receive(block, corner, 1) for corner in ("x", "y", "z", "xyz"))
    near, = barrier(jnp.concatenate([block, x, y, z]))
    xy, yz, zx = receive(y, "x", 1), receive(z, "y", 1), receive(x, "z", 1)
    near, = barrier(jnp.concatenate([near, swap(near)]))
    near = flat(near)
    done = work(near)
    xy, yz, zx, xyz, _ = barrier(xy, yz, zx, xyz, done)
    distant, = barrier(jnp.concatenate([xy, yz, zx, xyz]))
    return near, done, flat(distant), flat(swap(distant))


def scatter(near, distant, work):
    xy, yz, zx, xyz = jnp.split(distant.reshape(32, 8, -1), 4)
    own, x, y, z = jnp.split(near.reshape(32, 8, -1), 4)
    y_more, z_more, x_more = receive(xy, "x", 1), receive(yz, "y", 1), receive(zx, "z", 1)
    xyz = receive(xyz, "xyz", 1)
    x, y, z = (add(*pair).astype(bf16) for pair in ((x, x_more), (y, y_more), (z, z_more)))
    done = work(x_more)
    x, y, z = receive(x, "x", 1), receive(y, "y", 1), receive(z, "z", 1)
    x, y, z, xyz, done = barrier(x, y, z, xyz, done)
    blocks = trade(add(own, xyz, x, y, z).astype(bf16), 0)
    return jnp.sum(blocks.astype(f32), axis=0), done


def on_device(activations, enc_weight, enc_bias, thresholds, dec_weight, dec_bias):
    row_scale = 1.0 / math.sqrt(1024)
    own_rows = lax.all_to_all(activations, ("x", "yl"), split_axis=0, concat_axis=1, tiled=True)
    own_rows = own_rows.astype(f32)
    own_centered, = barrier((own_rows - dec_bias).astype(bf16))

    def encode(rows):
        pre_act, = barrier(jnp.dot(rows, enc_weight, preferred_element_type=f32) + enc_bias)
        gating = jax.nn.sigmoid((pre_act - thresholds) / band_width)
        code_values = pre_act * gating
        slopes = gating + pre_act * gating * (1.0 - gating) / band_width
        return barrier(code_values.astype(bf16), slopes, jnp.sum(code_values, axis=0))

    near, encoded, mine, theirs = gather(own_centered, encode)
    code_near, slopes_near, totals_near = encoded
    code_mine, slopes_mine, totals_mine = encode(mine)
    theirs, _ = barrier(theirs, code_mine)
    code_theirs, slopes_theirs, totals_theirs = encode(theirs)
    totals = totals_near + totals_mine + totals_theirs

    code_mine_all, code_theirs_all = barrier(
        jnp.concatenate([code_mine, code_near[:256]]),
        jnp.concatenate([code_theirs, code_near[256:]]),
    )
    recon_theirs = jnp.dot(code_theirs_all, dec_weight, preferred_element_type=f32).astype(bf16)
    recon_theirs = swap(recon_theirs[:256]), swap(recon_theirs[256:])
    recon_mine, = barrier(
        jnp.dot(code_mine_all, dec_weight, preferred_element_type=f32).astype(bf16)
    )
    recon_distant, = barrier(add(recon_mine[:256], recon_theirs[0]).astype(bf16))
    recon_mine, recon_distant = barrier(recon_mine, recon_distant)
    recon_near = add(recon_mine[256:], recon_theirs[1]).astype(bf16)

    def side_work(received):
        *rest, dec, _ = barrier(
            near, code_near, mine, theirs, code_mine, code_theirs, slopes_mine, slopes_theirs,
            dec_weight, received,
        )
        near_rows, code_rows, mine_rows, their_rows, mine_code, their_code, *slopes = rest
        row_norms = jnp.sqrt(jnp.sum(jnp.square(dec.astype(f32)), axis=1) + 1e-06)
        return (
            near_rows.T,
            code_rows.T,
            jnp.concatenate([mine_rows, their_rows]).T,
            jnp.concatenate([mine_code, their_code]).T,
            jnp.concatenate(slopes),
            sparsity_coeff * row_scale * row_norms,
            sparsity_coeff * row_scale * totals / row_norms,
        )

    recon, work = scatter(recon_near, recon_distant, side_work)
    near_t, code_near_t, distant_t, code_distant_t, slopes_distant, norm_grad, norm_scale = work
    recon_error = recon + dec_bias - own_rows
    own_delta, = barrier((recon_error * row_scale).astype(bf16))

    def preact_grad(delta, slopes):
        code_grad = lax.dot_general(
            delta, dec_weight, (((1,), (1,)), ((), ())), preferred_element_type=f32
        )
        return barrier(
            ((code_grad + norm_grad) * slopes).astype(bf16)
        )[0]

    def near_grad(delta):
        preact = preact_grad(delta, slopes_near)
        return jnp.dot(near_t, preact, preferred_element_type=f32).astype(bf16)

    delta_near, grad_enc, mine, theirs = gather(own_delta, near_grad)
    grad_dec = jnp.dot(code_near_t, delta_near, preferred_element_type=f32)
    grad_dec = (grad_dec + norm_scale[:, None] * dec_weight.astype(f32)).astype(bf16)
    grad_dec, = barrier(grad_dec)
    theirs, _ = barrier(theirs, grad_dec)
    delta, = barrier(jnp.concatenate([mine, theirs]))
    preact = preact_grad(delta, slopes_distant)
    grad_enc = grad_enc + jnp.dot(distant_t, preact, preferred_element_type=f32)
    grad_dec = grad_dec + jnp.dot(code_distant_t, delta, preferred_element_type=f32)
    return (grad_enc.astype(bf16), grad_dec.astype(bf16))


def solution(mesh):
    torus = Mesh(mesh.devices.reshape(4, 2, 2, 4, 2), MESH)
    dp, tensor = ("z", "yh", "core"), ("x", "yl")
    latents = dp + tensor
    in_specs = (P(dp, tensor), P(None, latents), P(latents), P(latents), P(latents, None), P())
    out_specs = (P(None, latents), P(latents, None))
    return jax.shard_map(
        on_device, mesh=torus, in_specs=in_specs, out_specs=out_specs, check_vma=False
    )
```

```python
import math

import jax
import jax.numpy as jnp
from jax import lax
from jax.sharding import Mesh, PartitionSpec as P

band_width = 0.1
sparsity_coeff = 0.5

bf16, f32 = jnp.bfloat16, jnp.float32
MESH = ("z", "yh", "core", "x", "yl")


def device(z, y, x, core):
    return (((z * 2 + y // 2) * 2 + core) * 4 + x) * 2 + y % 2


def receive(block, axes, pairing):
    pairs = []
    for z in range(4):
        for y in range(4):
            for x in range(4):
                for core in range(2):
                    partner = {"z": z, "y": y, "x": x}
                    for axis in axes:
                        partner[axis] ^= (1, 3)[(pairing + core) % 2]
                    pairs.append((device(core=core, **partner), device(z, y, x, core)))
    return lax.ppermute(block, MESH, pairs)


def cubes(pairing):
    groups = []
    for core in range(2):
        step = (1, 3)[(pairing + core) % 2]
        corners = (0, 1 if step == 3 else 2)
        pairs = [(corner, corner ^ step) for corner in corners]
        for zs in pairs:
            for ys in pairs:
                for xs in pairs:
                    groups.append([device(z, y, x, core) for z in zs for y in ys for x in xs])
    return groups


def trade(blocks, pairing):
    return lax.all_to_all(blocks, MESH, 0, 0, axis_index_groups=cubes(pairing))


def swap(block):
    return lax.ppermute(block, "core", [(0, 1), (1, 0)])


def barrier(*arrays):
    return lax.optimization_barrier(arrays)


def add(*blocks):
    return sum(block.astype(f32) for block in blocks)


def flat(block):
    return block.reshape(-1, block.shape[-1])


def gather(own, work):
    copies, = barrier(jnp.broadcast_to(own, (8, *own.shape)))
    block, = barrier(trade(copies, 0))
    x, y, z = (receive(block, axis, 1) for axis in "xyz")
    near, = barrier(jnp.concatenate([block, x, y, z]))
    xy, yz, zx = receive(y, "x", 1), receive(z, "y", 1), receive(x, "z", 1)
    xyz = receive(z, "xy", 1)
    near, = barrier(jnp.concatenate([near, swap(near)]))
    near = flat(near)
    done = work(near)
    xy, yz, zx, xyz, _ = barrier(xy, yz, zx, xyz, done)
    distant, = barrier(jnp.concatenate([xy, yz, zx, xyz]))
    return near, done, flat(distant), flat(swap(distant))


def scatter(near, distant, work):
    (own, x, y, z), (xy, yz, zx, xyz) = near, distant
    y_more, z_more, x_more = receive(xy, "x", 1), receive(yz, "y", 1), receive(zx, "z", 1)
    xyz = receive(xyz, "xyz", 1)
    x, y, z = (add(*pair).astype(bf16) for pair in ((x, x_more), (y, y_more), (z, z_more)))
    done = work(x_more)
    x, y, z = receive(x, "x", 1), receive(y, "y", 1), receive(z, "z", 1)
    x, y, z, xyz, done = barrier(x, y, z, xyz, done)
    blocks = trade(add(own, xyz, x, y, z).astype(bf16), 0)
    return jnp.sum(blocks.astype(f32), axis=0), done


def on_device(activations, enc_weight, enc_bias, thresholds, dec_weight, dec_bias):
    row_scale = 1.0 / math.sqrt(1024)
    own_rows = lax.all_to_all(activations, ("x", "yl"), split_axis=0, concat_axis=1, tiled=True)
    own_rows = own_rows.astype(f32)
    own_centered, = barrier((own_rows - dec_bias).astype(bf16))

    def encode(rows):
        pre_act, = barrier(jnp.dot(rows, enc_weight, preferred_element_type=f32) + enc_bias)
        gating = jax.nn.sigmoid((pre_act - thresholds) / band_width)
        code_values = pre_act * gating
        slopes = gating + pre_act * gating * (1.0 - gating) / band_width
        return barrier(code_values.astype(bf16), slopes, jnp.sum(code_values, axis=0))

    near, encoded, mine, theirs = gather(own_centered, encode)
    code_near, slopes_near, totals_near = encoded
    code_mine, slopes_mine, totals_mine = encode(mine)
    theirs, _ = barrier(theirs, code_mine)
    code_theirs, slopes_theirs, totals_theirs = encode(theirs)
    totals = totals_near + totals_mine + totals_theirs

    def decode(mine, theirs):
        theirs, mine = (
            barrier(jnp.dot(rows, dec_weight, preferred_element_type=f32).astype(bf16))[0]
            for rows in (theirs, mine)
        )
        pairs = zip(*(jnp.split(rows.reshape(32, 8, -1), 4) for rows in (mine, swap(theirs))))
        return barrier(*(add(*pair).astype(bf16) for pair in pairs))

    recon_near = decode(code_near[:256], code_near[256:])
    recon_distant = decode(code_mine, code_theirs)

    def side_work(received):
        *rest, dec, _ = barrier(
            near, code_near, mine, theirs, code_mine, code_theirs, slopes_mine, slopes_theirs,
            dec_weight, received,
        )
        near_rows, code_rows, mine_rows, their_rows, mine_code, their_code, *slopes = rest
        row_norms = jnp.sqrt(jnp.sum(jnp.square(dec.astype(f32)), axis=1) + 1e-06)
        return (
            near_rows.T,
            code_rows.T,
            jnp.concatenate([mine_rows, their_rows]).T,
            jnp.concatenate([mine_code, their_code]).T,
            *slopes,
            sparsity_coeff * row_scale * row_norms,
            sparsity_coeff * row_scale * totals / row_norms,
        )

    recon, work = scatter(recon_near, recon_distant, side_work)
    near_t, code_near_t, distant_t, code_distant_t, slopes_mine, slopes_theirs, *norms = work
    norm_grad, norm_scale = norms
    recon_error = recon + dec_bias - own_rows
    own_delta, = barrier((recon_error * row_scale).astype(bf16))

    def preact_grad(delta, slopes):
        code_grad = lax.dot_general(
            delta, dec_weight, (((1,), (1,)), ((), ())), preferred_element_type=f32
        )
        return barrier(
            ((code_grad + norm_grad) * slopes).astype(bf16)
        )[0]

    def near_grad(delta):
        preact = preact_grad(delta, slopes_near)
        return jnp.dot(near_t, preact, preferred_element_type=f32).astype(bf16)

    delta_near, grad_enc, mine, theirs = gather(own_delta, near_grad)
    grad_dec = jnp.dot(code_near_t, delta_near, preferred_element_type=f32)
    grad_dec = (grad_dec + norm_scale[:, None] * dec_weight.astype(f32)).astype(bf16)
    grad_dec, = barrier(grad_dec)
    preact_mine = preact_grad(mine, slopes_mine)
    theirs, _ = barrier(theirs, grad_dec)
    delta, = barrier(jnp.concatenate([mine, theirs]))
    preact, = barrier(jnp.concatenate([preact_mine, preact_grad(theirs, slopes_theirs)]))
    grad_enc = grad_enc + jnp.dot(distant_t, preact, preferred_element_type=f32)
    grad_dec = grad_dec + jnp.dot(code_distant_t, delta, preferred_element_type=f32)
    return (grad_enc.astype(bf16), grad_dec.astype(bf16))


def solution(mesh):
    torus = Mesh(mesh.devices.reshape(4, 2, 2, 4, 2), MESH)
    dp, tensor = ("z", "yh", "core"), ("x", "yl")
    latents = dp + tensor
    in_specs = (P(dp, tensor), P(None, latents), P(latents), P(latents), P(latents, None), P())
    out_specs = (P(None, latents), P(latents, None))
    return jax.shard_map(
        on_device, mesh=torus, in_specs=in_specs, out_specs=out_specs, check_vma=False
    )
```

```python
import math

import jax
import jax.numpy as jnp
from jax import lax
from jax.sharding import Mesh, PartitionSpec as P

band_width = 0.1
sparsity_coeff = 0.5

bf16, f32 = jnp.bfloat16, jnp.float32
MESH = ("z", "yh", "core", "x", "yl")


def device(z, y, x, core):
    return (((z * 2 + y // 2) * 2 + core) * 4 + x) * 2 + y % 2


def receive(block, axes, pairing):
    pairs = []
    for z in range(4):
        for y in range(4):
            for x in range(4):
                for core in range(2):
                    partner = {"z": z, "y": y, "x": x}
                    for axis in axes:
                        partner[axis] ^= (1, 3)[(pairing + core) % 2]
                    pairs.append((device(core=core, **partner), device(z, y, x, core)))
    return lax.ppermute(block, MESH, pairs)


def cubes(pairing):
    groups = []
    for core in range(2):
        step = (1, 3)[(pairing + core) % 2]
        corners = (0, 1 if step == 3 else 2)
        pairs = [(corner, corner ^ step) for corner in corners]
        for zs in pairs:
            for ys in pairs:
                for xs in pairs:
                    groups.append([device(z, y, x, core) for z in zs for y in ys for x in xs])
    return groups


def trade(blocks, pairing):
    return lax.all_to_all(blocks, MESH, 0, 0, axis_index_groups=cubes(pairing))


def swap(block):
    return lax.ppermute(block, "core", [(0, 1), (1, 0)])


def barrier(*arrays):
    return lax.optimization_barrier(arrays)


def add(*blocks):
    return sum(block.astype(f32) for block in blocks)


def flat(block):
    return block.reshape(-1, block.shape[-1])


def gather(own, work):
    copies, = barrier(jnp.broadcast_to(own, (8, *own.shape)))
    block, = barrier(trade(copies, 0))
    x, y, z = (receive(block, axis, 1) for axis in "xyz")
    near, = barrier(jnp.concatenate([block, x, y, z]))
    xy, yz, zx = receive(y, "x", 1), receive(z, "y", 1), receive(x, "z", 1)
    xyz = receive(z, "xy", 1)
    near, = barrier(jnp.concatenate([near, swap(near)]))
    near = flat(near)
    done = work(near)
    xy, yz, zx, xyz, _ = barrier(xy, yz, zx, xyz, done)
    distant, = barrier(jnp.concatenate([xy, yz, zx, xyz]))
    return near, done, flat(distant), flat(swap(distant))


def scatter(near, distant, work):
    (own, x, y, z), (xy, yz, zx, xyz) = near, distant
    y_more, z_more, x_more = receive(xy, "x", 1), receive(yz, "y", 1), receive(zx, "z", 1)
    xyz = receive(xyz, "xyz", 1)
    x, y, z = (add(*pair).astype(bf16) for pair in ((x, x_more), (y, y_more), (z, z_more)))
    done = work(x_more)
    x, y, z = receive(x, "x", 1), receive(y, "y", 1), receive(z, "z", 1)
    x, y, z, xyz, done = barrier(x, y, z, xyz, done)
    blocks = trade(add(own, xyz, x, y, z).astype(bf16), 0)
    return jnp.sum(blocks.astype(f32), axis=0), done


def on_device(activations, enc_weight, enc_bias, thresholds, dec_weight, dec_bias):
    row_scale = 1.0 / math.sqrt(1024)
    own_rows = lax.all_to_all(activations, ("x", "yl"), split_axis=0, concat_axis=1, tiled=True)
    own_rows = own_rows.astype(f32)
    own_centered, = barrier((own_rows - dec_bias).astype(bf16))

    def encode(rows):
        pre_act, = barrier(jnp.dot(rows, enc_weight, preferred_element_type=f32) + enc_bias)
        gating = jax.nn.sigmoid((pre_act - thresholds) / band_width)
        code_values = pre_act * gating
        slopes = gating + pre_act * gating * (1.0 - gating) / band_width
        return barrier(code_values.astype(bf16), slopes.astype(bf16), jnp.sum(code_values, axis=0))

    near, encoded, mine, theirs = gather(own_centered, encode)
    code_near, slopes_near, totals_near = encoded
    def decode(code_rows):
        return barrier(jnp.dot(code_rows, dec_weight, preferred_element_type=f32).astype(bf16))[0]

    def sums(mine, theirs):
        pairs = zip(*(jnp.split(rows.reshape(32, 8, -1), 4) for rows in (mine, swap(theirs))))
        return barrier(*(add(*pair).astype(bf16) for pair in pairs))

    recon_theirs = decode(code_near[256:])
    code_mine, slopes_mine, totals_mine = encode(mine)
    theirs, _, _ = barrier(theirs, code_mine, recon_theirs)
    code_theirs, slopes_theirs, totals_theirs = encode(theirs)
    totals = totals_near + totals_mine + totals_theirs
    recon_distant = sums(decode(code_mine), decode(code_theirs))
    recon_mine = decode(code_near[:256])
    recon_theirs, _ = barrier(recon_theirs, recon_distant)
    recon_near = sums(recon_mine, recon_theirs)

    def side_work(received):
        *rest, dec, _ = barrier(
            near, code_near, mine, theirs, code_mine, code_theirs, slopes_mine, slopes_theirs,
            dec_weight, received,
        )
        near_rows, code_rows, mine_rows, their_rows, mine_code, their_code, *slopes = rest
        row_norms = jnp.sqrt(jnp.sum(jnp.square(dec.astype(f32)), axis=1) + 1e-06)
        return (
            near_rows.T,
            code_rows.T,
            jnp.concatenate([mine_rows, their_rows]).T,
            jnp.concatenate([mine_code, their_code]).T,
            *slopes,
            sparsity_coeff * row_scale * row_norms,
            sparsity_coeff * row_scale * totals / row_norms,
        )

    recon, work = scatter(recon_near, recon_distant, side_work)
    near_t, code_near_t, distant_t, code_distant_t, slopes_mine, slopes_theirs, *norms = work
    norm_grad, norm_scale = norms
    recon_error = recon + dec_bias - own_rows
    own_delta, = barrier((recon_error * row_scale).astype(bf16))

    def preact_grad(delta, slopes):
        code_grad = lax.dot_general(
            delta, dec_weight, (((1,), (1,)), ((), ())), preferred_element_type=f32
        )
        return barrier(
            ((code_grad + norm_grad) * slopes).astype(bf16)
        )[0]

    def near_grad(delta):
        preact = preact_grad(delta, slopes_near)
        return jnp.dot(near_t, preact, preferred_element_type=f32).astype(bf16)

    delta_near, grad_enc, mine, theirs = gather(own_delta, near_grad)
    grad_dec = jnp.dot(code_near_t, delta_near, preferred_element_type=f32)
    grad_dec = (grad_dec + norm_scale[:, None] * dec_weight.astype(f32)).astype(bf16)
    grad_dec, = barrier(grad_dec)
    preact_mine = preact_grad(mine, slopes_mine)
    theirs, _ = barrier(theirs, grad_dec)
    delta, = barrier(jnp.concatenate([mine, theirs]))
    preact, = barrier(jnp.concatenate([preact_mine, preact_grad(theirs, slopes_theirs)]))
    grad_enc = grad_enc + jnp.dot(distant_t, preact, preferred_element_type=f32)
    grad_dec = grad_dec + jnp.dot(code_distant_t, delta, preferred_element_type=f32)
    return (grad_enc.astype(bf16), grad_dec.astype(bf16))


def solution(mesh):
    torus = Mesh(mesh.devices.reshape(4, 2, 2, 4, 2), MESH)
    dp, tensor = ("z", "yh", "core"), ("x", "yl")
    latents = dp + tensor
    in_specs = (P(dp, tensor), P(None, latents), P(latents), P(latents), P(latents, None), P())
    out_specs = (P(None, latents), P(latents, None))
    return jax.shard_map(
        on_device, mesh=torus, in_specs=in_specs, out_specs=out_specs, check_vma=False
    )
```

```python
import math

import jax
import jax.numpy as jnp
from jax import lax
from jax.sharding import Mesh, PartitionSpec as P

band_width = 0.1
sparsity_coeff = 0.5

bf16, f32 = jnp.bfloat16, jnp.float32
MESH = ("z", "yh", "core", "x", "yl")


def device(z, y, x, core):
    return (((z * 2 + y // 2) * 2 + core) * 4 + x) * 2 + y % 2


def receive(block, axes, pairing):
    pairs = []
    for z in range(4):
        for y in range(4):
            for x in range(4):
                for core in range(2):
                    partner = {"z": z, "y": y, "x": x}
                    for axis in axes:
                        partner[axis] ^= (1, 3)[(pairing + core) % 2]
                    pairs.append((device(core=core, **partner), device(z, y, x, core)))
    return lax.ppermute(block, MESH, pairs)


def cubes(pairing):
    groups = []
    for core in range(2):
        step = (1, 3)[(pairing + core) % 2]
        corners = (0, 1 if step == 3 else 2)
        pairs = [(corner, corner ^ step) for corner in corners]
        for zs in pairs:
            for ys in pairs:
                for xs in pairs:
                    groups.append([device(z, y, x, core) for z in zs for y in ys for x in xs])
    return groups


def trade(blocks, pairing):
    return lax.all_to_all(blocks, MESH, 0, 0, axis_index_groups=cubes(pairing))


def swap(block):
    return lax.ppermute(block, "core", [(0, 1), (1, 0)])


def barrier(*arrays):
    return lax.optimization_barrier(arrays)


def add(*blocks):
    return sum(block.astype(f32) for block in blocks)


def flat(block):
    return block.reshape(-1, block.shape[-1])


def gather(own, work):
    copies, = barrier(jnp.broadcast_to(own, (8, *own.shape)))
    block, = barrier(trade(copies, 0))
    x, y, z = (receive(block, axis, 1) for axis in "xyz")
    near, = barrier(jnp.concatenate([block, x, y, z]))
    xy, yz, zx = receive(y, "x", 1), receive(z, "y", 1), receive(x, "z", 1)
    xyz = receive(z, "xy", 1)
    near, = barrier(jnp.concatenate([near, swap(near)]))
    near = flat(near)
    done = work(near)
    xy, yz, zx, xyz, _ = barrier(xy, yz, zx, xyz, done)
    distant, = barrier(jnp.concatenate([xy, yz, zx, xyz]))
    return near, done, flat(distant), flat(swap(distant))


def sums(mine, theirs):
    pairs = zip(*(jnp.split(rows.reshape(32, 8, -1), 4) for rows in (mine, theirs)))
    return barrier(*(add(*pair).astype(bf16) for pair in pairs))


def scatter(near, distant, work):
    xy, yz, zx, xyz = distant
    y_more, z_more, x_more = receive(xy, "x", 1), receive(yz, "y", 1), receive(zx, "z", 1)
    xyz = receive(xyz, "xyz", 1)
    own, x, y, z = sums(*barrier(*near, y_more)[:2])
    x, y, z = (add(*pair).astype(bf16) for pair in ((x, x_more), (y, y_more), (z, z_more)))
    done = work(x_more)
    x, y, z = receive(x, "x", 1), receive(y, "y", 1), receive(z, "z", 1)
    x, y, z, xyz, done = barrier(x, y, z, xyz, done)
    blocks = trade(add(own, xyz, x, y, z).astype(bf16), 0)
    return jnp.sum(blocks.astype(f32), axis=0), done


def on_device(activations, enc_weight, enc_bias, thresholds, dec_weight, dec_bias):
    row_scale = 1.0 / math.sqrt(1024)
    own_rows = lax.all_to_all(activations, ("x", "yl"), split_axis=0, concat_axis=1, tiled=True)
    own_rows = own_rows.astype(f32)
    own_centered, = barrier((own_rows - dec_bias).astype(bf16))

    def encode(rows):
        pre_act, = barrier(jnp.dot(rows, enc_weight, preferred_element_type=f32) + enc_bias)
        gating = jax.nn.sigmoid((pre_act - thresholds) / band_width)
        code_values = pre_act * gating
        slopes = gating + pre_act * gating * (1.0 - gating) / band_width
        return barrier(code_values.astype(bf16), slopes, jnp.sum(code_values, axis=0))

    near, encoded, mine, theirs = gather(own_centered, encode)
    code_near, slopes_near, totals_near = encoded
    code_mine, slopes_mine, totals_mine = encode(mine)
    theirs, _ = barrier(theirs, code_mine)
    code_theirs, slopes_theirs, totals_theirs = encode(theirs)
    totals = totals_near + totals_mine + totals_theirs

    def decode(mine, theirs):
        theirs, mine = (
            barrier(jnp.dot(rows, dec_weight, preferred_element_type=f32).astype(bf16))[0]
            for rows in (theirs, mine)
        )
        return mine, swap(theirs)

    recon_near = decode(code_near[:256], code_near[256:])
    recon_distant = sums(*decode(code_mine, code_theirs))

    def side_work(received):
        *rest, dec, _ = barrier(
            near, code_near, mine, theirs, code_mine, code_theirs, slopes_mine, slopes_theirs,
            dec_weight, received,
        )
        near_rows, code_rows, mine_rows, their_rows, mine_code, their_code, *slopes = rest
        row_norms = jnp.sqrt(jnp.sum(jnp.square(dec.astype(f32)), axis=1) + 1e-06)
        return (
            near_rows.T,
            code_rows.T,
            jnp.concatenate([mine_rows, their_rows]).T,
            jnp.concatenate([mine_code, their_code]).T,
            *slopes,
            sparsity_coeff * row_scale * row_norms,
            sparsity_coeff * row_scale * totals / row_norms,
        )

    recon, work = scatter(recon_near, recon_distant, side_work)
    near_t, code_near_t, distant_t, code_distant_t, slopes_mine, slopes_theirs, *norms = work
    norm_grad, norm_scale = norms
    recon_error = recon + dec_bias - own_rows
    own_delta, = barrier((recon_error * row_scale).astype(bf16))

    def preact_grad(delta, slopes):
        code_grad = lax.dot_general(
            delta, dec_weight, (((1,), (1,)), ((), ())), preferred_element_type=f32
        )
        return barrier(
            ((code_grad + norm_grad) * slopes).astype(bf16)
        )[0]

    def near_grad(delta):
        preact = preact_grad(delta, slopes_near)
        return jnp.dot(near_t, preact, preferred_element_type=f32).astype(bf16)

    delta_near, grad_enc, mine, theirs = gather(own_delta, near_grad)
    grad_dec = jnp.dot(code_near_t, delta_near, preferred_element_type=f32)
    grad_dec = (grad_dec + norm_scale[:, None] * dec_weight.astype(f32)).astype(bf16)
    grad_dec, = barrier(grad_dec)
    preact_mine = preact_grad(mine, slopes_mine)
    theirs, _ = barrier(theirs, grad_dec)
    delta, = barrier(jnp.concatenate([mine, theirs]))
    preact, = barrier(jnp.concatenate([preact_mine, preact_grad(theirs, slopes_theirs)]))
    grad_enc = grad_enc + jnp.dot(distant_t, preact, preferred_element_type=f32)
    grad_dec = grad_dec + jnp.dot(code_distant_t, delta, preferred_element_type=f32)
    return (grad_enc.astype(bf16), grad_dec.astype(bf16))


def solution(mesh):
    torus = Mesh(mesh.devices.reshape(4, 2, 2, 4, 2), MESH)
    dp, tensor = ("z", "yh", "core"), ("x", "yl")
    latents = dp + tensor
    in_specs = (P(dp, tensor), P(None, latents), P(latents), P(latents), P(latents, None), P())
    out_specs = (P(None, latents), P(latents, None))
    return jax.shard_map(
        on_device, mesh=torus, in_specs=in_specs, out_specs=out_specs, check_vma=False
    )
```

```python
import math

import jax
import jax.numpy as jnp
from jax import lax
from jax.sharding import Mesh, PartitionSpec as P

band_width = 0.1
sparsity_coeff = 0.5

bf16, f32 = jnp.bfloat16, jnp.float32
MESH = ("z", "yh", "core", "x", "yl")


def device(z, y, x, core):
    return (((z * 2 + y // 2) * 2 + core) * 4 + x) * 2 + y % 2


def receive(block, axes, pairing):
    pairs = []
    for z in range(4):
        for y in range(4):
            for x in range(4):
                for core in range(2):
                    partner = {"z": z, "y": y, "x": x}
                    for axis in axes:
                        partner[axis] ^= (1, 3)[(pairing + core) % 2]
                    pairs.append((device(core=core, **partner), device(z, y, x, core)))
    return lax.ppermute(block, MESH, pairs)


def cubes(pairing):
    groups = []
    for core in range(2):
        step = (1, 3)[(pairing + core) % 2]
        corners = (0, 1 if step == 3 else 2)
        pairs = [(corner, corner ^ step) for corner in corners]
        for zs in pairs:
            for ys in pairs:
                for xs in pairs:
                    groups.append([device(z, y, x, core) for z in zs for y in ys for x in xs])
    return groups


def trade(blocks, pairing):
    return lax.all_to_all(blocks, MESH, 0, 0, axis_index_groups=cubes(pairing))


def swap(block):
    return lax.ppermute(block, "core", [(0, 1), (1, 0)])


def barrier(*arrays):
    return lax.optimization_barrier(arrays)


def add(*blocks):
    return sum(block.astype(f32) for block in blocks)


def flat(block):
    return block.reshape(-1, block.shape[-1])


def gather(own, work):
    copies, = barrier(jnp.broadcast_to(own, (8, *own.shape)))
    block, = barrier(trade(copies, 0))
    x, y, z = (receive(block, axis, 1) for axis in "xyz")
    near, = barrier(jnp.concatenate([block, x, y, z]))
    xy, yz, zx = receive(y, "x", 1), receive(z, "y", 1), receive(x, "z", 1)
    xyz = receive(z, "xy", 1)
    near, = barrier(jnp.concatenate([near, swap(near)]))
    near = flat(near)
    done = work(near)
    xy, yz, zx, xyz, _ = barrier(xy, yz, zx, xyz, done)
    distant, = barrier(jnp.concatenate([xy, yz, zx, xyz]))
    return near, done, flat(distant), flat(swap(distant))


def scatter(near, distant, work):
    (own, x, y, z), (xy, yz, zx, xyz) = near, distant
    y_more, z_more, x_more = receive(xy, "x", 1), receive(yz, "y", 1), receive(zx, "z", 1)
    xyz = receive(xyz, "xyz", 1)
    x, y, z = (add(*pair).astype(bf16) for pair in ((x, x_more), (y, y_more), (z, z_more)))
    done = work(x_more)
    x, y, z = receive(x, "x", 1), receive(y, "y", 1), receive(z, "z", 1)
    x, y, z, xyz, done = barrier(x, y, z, xyz, done)
    blocks = trade(add(own, xyz, x, y, z).astype(bf16), 0)
    return jnp.sum(blocks.astype(f32), axis=0), done


def on_device(activations, enc_weight, enc_bias, thresholds, dec_weight, dec_bias):
    row_scale = 1.0 / math.sqrt(1024)
    own_rows = lax.all_to_all(activations, ("x", "yl"), split_axis=0, concat_axis=1, tiled=True)
    own_rows = own_rows.astype(f32)
    own_centered, = barrier((own_rows - dec_bias).astype(bf16))

    def encode(rows):
        pre_act, = barrier(jnp.dot(rows, enc_weight, preferred_element_type=f32) + enc_bias)
        code_values = pre_act * jax.nn.sigmoid((pre_act - thresholds) / band_width)
        return barrier(code_values.astype(bf16), pre_act, jnp.sum(code_values, axis=0))

    def slopes_of(pre_act):
        gating = jax.nn.sigmoid((pre_act - thresholds) / band_width)
        return gating + pre_act * gating * (1.0 - gating) / band_width

    near, encoded, mine, theirs = gather(own_centered, encode)
    code_near, pre_near, totals_near = encoded
    code_mine, pre_mine, totals_mine = encode(mine)
    theirs, _ = barrier(theirs, code_mine)
    code_theirs, pre_theirs, totals_theirs = encode(theirs)
    totals = totals_near + totals_mine + totals_theirs

    def decode(mine, theirs):
        theirs, mine = (
            barrier(jnp.dot(rows, dec_weight, preferred_element_type=f32).astype(bf16))[0]
            for rows in (theirs, mine)
        )
        pairs = zip(*(jnp.split(rows.reshape(32, 8, -1), 4) for rows in (mine, swap(theirs))))
        return barrier(*(add(*pair).astype(bf16) for pair in pairs))

    recon_near = decode(code_near[:256], code_near[256:])
    recon_distant = decode(code_mine, code_theirs)

    def side_work(received):
        *rest, dec, _ = barrier(
            near, code_near, mine, theirs, code_mine, code_theirs, pre_near, pre_mine, pre_theirs,
            dec_weight, received,
        )
        near_rows, code_rows, mine_rows, their_rows, mine_code, their_code, *pre_acts = rest
        row_norms = jnp.sqrt(jnp.sum(jnp.square(dec.astype(f32)), axis=1) + 1e-06)
        return (
            near_rows.T,
            code_rows.T,
            jnp.concatenate([mine_rows, their_rows]).T,
            jnp.concatenate([mine_code, their_code]).T,
            *(slopes_of(pre_act) for pre_act in pre_acts),
            sparsity_coeff * row_scale * row_norms,
            sparsity_coeff * row_scale * totals / row_norms,
        )

    recon, work = scatter(recon_near, recon_distant, side_work)
    near_t, code_near_t, distant_t, code_distant_t, *slopes, norm_grad, norm_scale = work
    slopes_near, slopes_mine, slopes_theirs = slopes
    recon_error = recon + dec_bias - own_rows
    own_delta, = barrier((recon_error * row_scale).astype(bf16))

    def preact_grad(delta, slopes):
        code_grad = lax.dot_general(
            delta, dec_weight, (((1,), (1,)), ((), ())), preferred_element_type=f32
        )
        return barrier(
            ((code_grad + norm_grad) * slopes).astype(bf16)
        )[0]

    def near_grad(delta):
        preact = preact_grad(delta, slopes_near)
        return jnp.dot(near_t, preact, preferred_element_type=f32).astype(bf16)

    delta_near, grad_enc, mine, theirs = gather(own_delta, near_grad)
    grad_dec = jnp.dot(code_near_t, delta_near, preferred_element_type=f32)
    grad_dec = (grad_dec + norm_scale[:, None] * dec_weight.astype(f32)).astype(bf16)
    grad_dec, = barrier(grad_dec)
    preact_mine = preact_grad(mine, slopes_mine)
    theirs, _ = barrier(theirs, grad_dec)
    delta, = barrier(jnp.concatenate([mine, theirs]))
    preact, = barrier(jnp.concatenate([preact_mine, preact_grad(theirs, slopes_theirs)]))
    grad_enc = grad_enc + jnp.dot(distant_t, preact, preferred_element_type=f32)
    grad_dec = grad_dec + jnp.dot(code_distant_t, delta, preferred_element_type=f32)
    return (grad_enc.astype(bf16), grad_dec.astype(bf16))


def solution(mesh):
    torus = Mesh(mesh.devices.reshape(4, 2, 2, 4, 2), MESH)
    dp, tensor = ("z", "yh", "core"), ("x", "yl")
    latents = dp + tensor
    in_specs = (P(dp, tensor), P(None, latents), P(latents), P(latents), P(latents, None), P())
    out_specs = (P(None, latents), P(latents, None))
    return jax.shard_map(
        on_device, mesh=torus, in_specs=in_specs, out_specs=out_specs, check_vma=False
    )
```

```python
import math

import jax
import jax.numpy as jnp
from jax import lax
from jax.sharding import Mesh, PartitionSpec as P

band_width = 0.1
sparsity_coeff = 0.5

bf16, f32 = jnp.bfloat16, jnp.float32
MESH = ("z", "yh", "core", "x", "yl")


def device(z, y, x, core):
    return (((z * 2 + y // 2) * 2 + core) * 4 + x) * 2 + y % 2


def receive(block, axes, pairing):
    pairs = []
    for z in range(4):
        for y in range(4):
            for x in range(4):
                for core in range(2):
                    partner = {"z": z, "y": y, "x": x}
                    for axis in axes:
                        partner[axis] ^= (1, 3)[(pairing + core) % 2]
                    pairs.append((device(core=core, **partner), device(z, y, x, core)))
    return lax.ppermute(block, MESH, pairs)


def cubes(pairing):
    groups = []
    for core in range(2):
        step = (1, 3)[(pairing + core) % 2]
        corners = (0, 1 if step == 3 else 2)
        pairs = [(corner, corner ^ step) for corner in corners]
        for zs in pairs:
            for ys in pairs:
                for xs in pairs:
                    groups.append([device(z, y, x, core) for z in zs for y in ys for x in xs])
    return groups


def trade(blocks, pairing):
    return lax.all_to_all(blocks, MESH, 0, 0, axis_index_groups=cubes(pairing))


def swap(block):
    return lax.ppermute(block, "core", [(0, 1), (1, 0)])


def barrier(*arrays):
    return lax.optimization_barrier(arrays)


def add(*blocks):
    return sum(block.astype(f32) for block in blocks)


def flat(block):
    return block.reshape(-1, block.shape[-1])


def gather(own, work):
    copies, = barrier(jnp.broadcast_to(own, (8, *own.shape)))
    block, = barrier(trade(copies, 0))
    x, y, z = (receive(block, axis, 1) for axis in "xyz")
    near, = barrier(jnp.concatenate([block, x, y, z]))
    xy, yz, zx = receive(y, "x", 1), receive(z, "y", 1), receive(x, "z", 1)
    xyz = receive(z, "xy", 1)
    near, = barrier(jnp.concatenate([near, swap(near)]))
    near = flat(near)
    done = work(near)
    xy, yz, zx, xyz, _ = barrier(xy, yz, zx, xyz, done)
    distant, = barrier(jnp.concatenate([xy, yz, zx, xyz]))
    return near, done, flat(distant), flat(swap(distant))


def scatter(near, distant, work):
    (own, x, y, z), (xy, yz, zx, xyz) = near, distant
    y_more, z_more, x_more = receive(xy, "x", 1), receive(yz, "y", 1), receive(zx, "z", 1)
    xyz = receive(xyz, "xyz", 1)
    x, y, z = (add(*pair).astype(bf16) for pair in ((x, x_more), (y, y_more), (z, z_more)))
    done = work(x_more)
    x, y, z = receive(x, "x", 1), receive(y, "y", 1), receive(z, "z", 1)
    x, y, z, xyz, done = barrier(x, y, z, xyz, done)
    blocks = trade(add(own, xyz, x, y, z).astype(bf16), 0)
    return jnp.sum(blocks.astype(f32), axis=0), done


def on_device(activations, enc_weight, enc_bias, thresholds, dec_weight, dec_bias):
    row_scale = 1.0 / math.sqrt(1024)
    own_rows = lax.all_to_all(activations, ("x", "yl"), split_axis=0, concat_axis=1, tiled=True)
    own_rows = own_rows.astype(f32)
    own_centered, = barrier((own_rows - dec_bias).astype(bf16))

    def encode(rows):
        pre_act, = barrier(jnp.dot(rows, enc_weight, preferred_element_type=f32) + enc_bias)
        gating = jax.nn.sigmoid((pre_act - thresholds) / band_width)
        code_values = pre_act * gating
        slopes = gating + pre_act * gating * (1.0 - gating) / band_width
        return barrier(code_values.astype(bf16), slopes, jnp.sum(code_values, axis=0))

    near, encoded, mine, theirs = gather(own_centered, encode)
    code_near, slopes_near, totals_near = encoded
    code_mine, slopes_mine, totals_mine = encode(mine)
    theirs, _ = barrier(theirs, code_mine)
    code_theirs, slopes_theirs, totals_theirs = encode(theirs)
    totals = totals_near + totals_mine + totals_theirs

    def decode(mine, theirs, parts):
        theirs, mine = (
            barrier(jnp.dot(rows, dec_weight, preferred_element_type=f32).astype(bf16))[0]
            for rows in (theirs, mine)
        )
        blocks = ()
        for part, other in zip(jnp.split(mine, parts), jnp.split(theirs, parts)):
            pairs = zip(
                *(jnp.split(rows.reshape(-1, 8, rows.shape[1]), 4 // parts) for rows in (part, swap(other)))
            )
            sums = tuple(add(*pair).astype(bf16) for pair in pairs)
            if blocks:
                *sums, _ = barrier(*sums, blocks)
            blocks += barrier(*sums) if len(blocks) == 0 else tuple(sums)
        return blocks

    recon_near = decode(code_near[:256], code_near[256:], 1)
    recon_distant = decode(code_mine, code_theirs, 2)

    def side_work(received):
        *rest, dec, _ = barrier(
            near, code_near, mine, theirs, code_mine, code_theirs, slopes_mine, slopes_theirs,
            dec_weight, received,
        )
        near_rows, code_rows, mine_rows, their_rows, mine_code, their_code, *slopes = rest
        row_norms = jnp.sqrt(jnp.sum(jnp.square(dec.astype(f32)), axis=1) + 1e-06)
        return (
            near_rows.T,
            code_rows.T,
            jnp.concatenate([mine_rows, their_rows]).T,
            jnp.concatenate([mine_code, their_code]).T,
            *slopes,
            sparsity_coeff * row_scale * row_norms,
            sparsity_coeff * row_scale * totals / row_norms,
        )

    recon, work = scatter(recon_near, recon_distant, side_work)
    near_t, code_near_t, distant_t, code_distant_t, slopes_mine, slopes_theirs, *norms = work
    norm_grad, norm_scale = norms
    recon_error = recon + dec_bias - own_rows
    own_delta, = barrier((recon_error * row_scale).astype(bf16))

    def preact_grad(delta, slopes):
        code_grad = lax.dot_general(
            delta, dec_weight, (((1,), (1,)), ((), ())), preferred_element_type=f32
        )
        return barrier(
            ((code_grad + norm_grad) * slopes).astype(bf16)
        )[0]

    def near_grad(delta):
        preact = preact_grad(delta, slopes_near)
        return jnp.dot(near_t, preact, preferred_element_type=f32).astype(bf16)

    delta_near, grad_enc, mine, theirs = gather(own_delta, near_grad)
    grad_dec = jnp.dot(code_near_t, delta_near, preferred_element_type=f32)
    grad_dec = (grad_dec + norm_scale[:, None] * dec_weight.astype(f32)).astype(bf16)
    grad_dec, = barrier(grad_dec)
    preact_mine = preact_grad(mine, slopes_mine)
    theirs, _ = barrier(theirs, grad_dec)
    delta, = barrier(jnp.concatenate([mine, theirs]))
    preact, = barrier(jnp.concatenate([preact_mine, preact_grad(theirs, slopes_theirs)]))
    grad_enc = grad_enc + jnp.dot(distant_t, preact, preferred_element_type=f32)
    grad_dec = grad_dec + jnp.dot(code_distant_t, delta, preferred_element_type=f32)
    return (grad_enc.astype(bf16), grad_dec.astype(bf16))


def solution(mesh):
    torus = Mesh(mesh.devices.reshape(4, 2, 2, 4, 2), MESH)
    dp, tensor = ("z", "yh", "core"), ("x", "yl")
    latents = dp + tensor
    in_specs = (P(dp, tensor), P(None, latents), P(latents), P(latents), P(latents, None), P())
    out_specs = (P(None, latents), P(latents, None))
    return jax.shard_map(
        on_device, mesh=torus, in_specs=in_specs, out_specs=out_specs, check_vma=False
    )
```
